256 devices in a mesh: row: 16 (over y, z_hi), col: 16 (over x, z_lo, core).
Axes of the slice: x: 4, y: 4, z: 8 (z_hi: 4, z_lo: 2; z = z_hi * 2 + z_lo), core: 2. Of those that a mesh axis runs over, the one named last changes fastest.
Arguments:
- object_tiles: float32 [2, 2, 6144, 6144], P(None, None, 'row', 'col'), may hold values from -4 to 4
- probe_field: float32 [2, 128, 128], replicated, may hold values from -4 to 4
- prop_phase: float32 [128, 128], replicated, may hold values from -3.140625 to 3.140625
- intensity: float32 [2048, 128, 128], P(('row', 'col')), may hold values from 0 to 2
- positions: int32 [2048, 2], P(('row', 'col')), may hold values from 0 to 383
- counts: int32 [16, 16], P('row'), may hold values from 1 to 8, as said below
Outputs:
- object_new: float32 [2, 2, 6144, 6144], P(None, None, 'row', 'col')
The draws below stay inside these ranges and needn't reach their ends.
Inputs may be any that keep to these rules, and one draw needn't show every extreme that they name: `counts`: in each row of the tile grid, in every aligned group of four tile columns 4j to 4j + 3, exactly two entries equal 8, and they sit at columns 4j and 4j + 1, or 4j + 2 and 4j + 3, or 4j and 4j + 2, or 4j + 1 and 4j + 3; the other two lie between 1 and 4.
All inputs are finite; a program needn't handle non-finite values.
Results may differ from the reference program's by a relative error of at most 0.0003.
Values sent between devices are 32-bit elements; how exact they have to be, the bound alone decides.
No kernel may reach another device: no remote copies, remote signals or barrier semaphores. Data moves between devices by JAX's collectives and lax.ppermute only.
A program may use at most 64 MiB of HBM per device.

```python
import jax
import jax.numpy as jnp
from jax import lax

TILE = 384
FRAME = 128
FR_DEV = 8
ITERS = 2
KEEP = 4
OBJ_ROWS = 6144
OBJ_COLS = 6144
FRAMES = 2048
N_ROW = 16
N_COL = 16


def draw_counts(key, part):
    pick_key = jax.random.fold_in(key, 11)
    light_key = jax.random.fold_in(key, 23)
    patterns = jnp.array([[1, 1, 0, 0], [0, 0, 1, 1], [1, 0, 1, 0], [0, 1, 0, 1]], dtype=jnp.int32)
    picks = jax.random.randint(pick_key, (N_ROW, N_COL // 4), 0, 4)
    busy_mask = patterns[picks].reshape(N_ROW, N_COL)
    light_load = jax.random.randint(light_key, (N_ROW, N_COL), 1, KEEP + 1)
    return jnp.where(busy_mask > 0, FR_DEV, light_load).astype(jnp.int32)


def with_ends(result, rng, low, largest):
    dims = result.shape
    index_at = [jax.random.randint(jax.random.fold_in(rng, axis), (), 0, dims[axis]) for axis in range(len(dims))]
    result = result.at[tuple(index_at)].set(low)
    longest = dims.index(max(dims))
    index_at[longest] = (index_at[longest] + 1) % dims[longest]
    return result.at[tuple(index_at)].set(largest)


def shard_levels(rng, dims, cuts, low, high):
    def one(position, parts):
        heights = jax.random.uniform(jax.random.fold_in(jax.random.fold_in(rng, 6), position), (parts,), jnp.float32, low / len(cuts), high / len(cuts))
        return jnp.repeat(jnp.exp(heights), dims[position] // parts).reshape((-1,) + (1,) * (len(dims) - position - 1))

    level = one(*cuts[0])
    for cut in cuts[1:]:
        level = level * one(*cut)
    return level


def normal_values(stream_key, extent, scale, limit, pieces=(), kind=jnp.bfloat16):
    drawn = jax.random.normal(stream_key, extent, jnp.float32) * scale
    if len(pieces) > 0:
        drawn = shard_levels(stream_key, extent, pieces, -0.22, 0.18) * drawn
    return jnp.clip(drawn, min=-limit, max=limit).astype(kind)


def setup_inputs(seed: int = 0) -> dict:
    keys = jax.random.split(jax.random.key(seed), 7)
    object_tiles = normal_values(keys[0], (2, 2, OBJ_ROWS, OBJ_COLS), 0.7, 4.0, ((2, 16), (3, 16)), jnp.float32)
    probe_field = normal_values(keys[1], (2, FRAME, FRAME), 0.7, 4.0, (), jnp.float32)
    prop_phase = jnp.clip(jax.random.uniform(keys[2], (FRAME, FRAME), jnp.float32, -3.140625, 3.140625), -3.140625, 3.140625)
    intensity = jnp.clip(2.0 * jax.random.uniform(keys[3], (FRAMES, FRAME, FRAME), jnp.float32) ** shard_levels(keys[3], (FRAMES, FRAME, FRAME), ((0, 256),), -0.2, 0.2), 0.0, 2.0)
    positions = with_ends(jax.random.randint(keys[4], (FRAMES, 2), 0, TILE), jax.random.fold_in(keys[4], 1), 0, TILE - 1).astype(jnp.int32)
    counts = draw_counts(jax.random.fold_in(keys[6], 71), 0)
    return dict(object_tiles=object_tiles, probe_field=probe_field, prop_phase=prop_phase, intensity=intensity, positions=positions, counts=counts)


step_size = 0.2


def frame_gradient(first_slice, second_slice, probe_wave, kernel, measured):
    lit_wave = probe_wave * first_slice
    inner_wave = jnp.fft.ifft2(kernel * jnp.fft.fft2(lit_wave, norm="ortho"), norm="ortho")
    far_field = jnp.fft.fft2(inner_wave * second_slice, norm="ortho")
    misfit = jnp.real(far_field) ** 2 + jnp.imag(far_field) ** 2 - measured
    back_field = jnp.fft.ifft2(misfit * far_field, norm="ortho")
    grad_second = jnp.conj(inner_wave) * back_field
    carried = jnp.fft.fft2(jnp.conj(second_slice) * back_field, norm="ortho")
    near_field = jnp.fft.ifft2(jnp.conj(kernel) * carried, norm="ortho")
    grad_first = jnp.conj(probe_wave) * near_field
    return jnp.stack([jnp.stack([jnp.real(grad_first), jnp.imag(grad_first)]),
                      jnp.stack([jnp.real(grad_second), jnp.imag(grad_second)])])


def reference(object_tiles, probe_field, prop_phase, intensity, positions, counts):
    padding = ((0, 0), (0, 0), (0, FRAME), (0, FRAME))
    padded = jnp.pad(object_tiles, padding)
    frame_ids = jnp.arange(FRAMES, dtype=jnp.int32)
    device_ids = frame_ids // FR_DEV
    grid_rows = device_ids // N_COL
    grid_cols = device_ids % N_COL
    active = ((frame_ids % FR_DEV) < counts[grid_rows, grid_cols]).astype(jnp.float32)
    top_rows = (grid_rows * TILE + positions[:, 0]).astype(jnp.int32)
    left_cols = (grid_cols * TILE + positions[:, 1]).astype(jnp.int32)
    probe_wave = lax.complex(probe_field[0], probe_field[1])
    kernel = lax.complex(jnp.cos(prop_phase), jnp.sin(prop_phase))
    for iteration in range(ITERS):
        source = padded

        def accumulate(grad_total, scan_item):
            top_row, left_col, weight, measured = scan_item
            corner_at = (jnp.int32(0), jnp.int32(0), top_row, left_col)
            patch_cut = lax.dynamic_slice(source, corner_at, (2, 2, FRAME, FRAME))
            first_slice = lax.complex(patch_cut[0, 0], patch_cut[0, 1])
            second_slice = lax.complex(patch_cut[1, 0], patch_cut[1, 1])
            gradient = frame_gradient(first_slice, second_slice, probe_wave, kernel, measured) * weight
            current = lax.dynamic_slice(grad_total, corner_at, (2, 2, FRAME, FRAME))
            return lax.dynamic_update_slice(grad_total, current + gradient, corner_at), None

        grad_total, unused = lax.scan(accumulate, jnp.zeros_like(source), (top_rows, left_cols, active, intensity))
        updated = source[:, :, :OBJ_ROWS, :OBJ_COLS] - step_size * grad_total[:, :, :OBJ_ROWS, :OBJ_COLS]
        padded = jnp.pad(updated, padding)
    return padded[:, :, :OBJ_ROWS, :OBJ_COLS]
```

```python
import functools

import numpy as np
import jax
import jax.numpy as jnp
from jax import lax
from jax.experimental import pallas as pl
from jax.experimental.pallas import tpu as pltpu
from jax.sharding import PartitionSpec as P
import ml_dtypes

ITERS = 2
STEP = 0.2
B = 128


def dft_tables():
    k = np.arange(B)
    phase = (np.outer(k, k) % B) * (2.0 * np.pi / B)
    c, s = np.cos(phase) / np.sqrt(B), -np.sin(phase) / np.sqrt(B)
    forward = np.block([[c, s], [-s, c]]).astype(np.float32)
    parts = []
    for full in (forward, forward.T):
        high = full.astype(ml_dtypes.bfloat16)
        low = (full - high.astype(np.float32)).astype(ml_dtypes.bfloat16)
        parts += [high, low]
    return np.stack(parts)


def split(x):
    high = x.astype(jnp.bfloat16)
    low = (x - high.astype(jnp.float32)).astype(jnp.bfloat16)
    return high, low


def dot(a, b):
    return jnp.dot(a, b, preferred_element_type=jnp.float32)


def right_mul(x, tab, at):
    high, low = split(x)
    t_high, t_low = tab[at], tab[at + 1]
    return dot(high, t_high) + (dot(low, t_high) + dot(high, t_low))


def left_mul(x, tab, at):
    high, low = split(x)
    t_high, t_low = tab[at], tab[at + 1]
    return dot(t_high, high) + (dot(t_high, low) + dot(t_low, high))


def rows_to_cols(y):
    top = jnp.concatenate([y[:B, :B], y[B:, :B]], axis=1)
    bottom = jnp.concatenate([y[:B, B:], y[B:, B:]], axis=1)
    return jnp.concatenate([top, bottom], axis=0)


def transform(re, im, tab, inverse):
    first, second = (2, 0) if inverse else (0, 2)
    x = jnp.concatenate(
        [jnp.concatenate([re[0], im[0]], axis=1), jnp.concatenate([re[1], im[1]], axis=1)], axis=0
    )
    y = rows_to_cols(right_mul(x, tab, first))
    z = left_mul(y, tab, second)
    return [z[:B, :B], z[:B, B:]], [z[B:, :B], z[B:, B:]]


PIECES = (
    ("core", ((1, 1), (1, 2), (2, 1), (2, 2))),
    ("top", ((0, 1), (0, 2))),
    ("left", ((1, 0), (2, 0))),
    ("first", ((0, 0),)),
    ("side", ((1, 3), (2, 3))),
    ("bottom", ((3, 1), (3, 2))),
    ("low", ((3, 0),)),
    ("ends", ((0, 3), (3, 3))),
)


def frames_kernel(last, pos_ref, cnt_ref, *refs):
    pieces, refs = refs[: len(PIECES)], refs[len(PIECES) :]
    inten_ref, probe_ref, kern_ref, tab = refs[:4]
    outs, (ext, grad, sems) = refs[4:-3], refs[-3:]
    copies = []
    for ref, (_, places) in zip(pieces, PIECES):
        for number, (rb, cb) in enumerate(places):
            copies.append(pltpu.make_async_copy(ref.at[number], ext.at[rb, cb], sems.at[rb * 4 + cb]))
    for c in copies:
        c.start()
    grad[...] = jnp.zeros_like(grad)
    for c in copies:
        c.wait()
    rows = lax.broadcasted_iota(jnp.int32, (B, B), 0)
    cols = lax.broadcasted_iota(jnp.int32, (B, B), 1)
    count = cnt_ref[0]

    def where_is(f):
        t, l = pos_ref[f, 0], pos_ref[f, 1]
        return t // B, lax.rem(t, B), l // B, lax.rem(l, B)

    def window(f):
        tb, ts, lb, ls = where_is(f)
        rm, cm = rows >= ts, cols >= ls

        def plane(k):
            upper = jnp.where(cm, ext[tb, lb, k], ext[tb, lb + 1, k])
            lower = jnp.where(cm, ext[tb + 1, lb, k], ext[tb + 1, lb + 1, k])
            return jnp.where(rm, upper, lower)

        return plane

    def probe(f):
        tb, ts, lb, ls = where_is(f)
        return [pltpu.roll(pltpu.roll(probe_ref[k], ts, 0), ls, 1) for k in range(2)]

    def add_back(f, planes):
        tb, ts, lb, ls = where_is(f)
        rm, cm = rows >= ts, cols >= ls
        zero = jnp.zeros((B, B), jnp.float32)
        for k, g in enumerate(planes):
            upper = jnp.where(rm, g, zero)
            lower = g - upper
            for db, part in ((0, upper), (1, lower)):
                left = jnp.where(cm, part, zero)
                grad[tb + db, lb, k] += left
                grad[tb + db, lb + 1, k] += part - left

    def pair(p, carry):
        fs = [2 * p, 2 * p + 1]
        win = [window(f) for f in fs]
        pr = [probe(f) for f in fs]
        o1r, o1i = [w(0) for w in win], [w(1) for w in win]
        ar = [pr[j][0] * o1r[j] - pr[j][1] * o1i[j] for j in range(2)]
        ai = [pr[j][0] * o1i[j] + pr[j][1] * o1r[j] for j in range(2)]
        fr, fi = transform(ar, ai, tab, False)
        kr, ki = kern_ref[0], kern_ref[1]
        mr = [kr * fr[j] - ki * fi[j] for j in range(2)]
        mi = [kr * fi[j] + ki * fr[j] for j in range(2)]
        br, bi = transform(mr, mi, tab, True)
        o2r, o2i = [w(2) for w in win], [w(3) for w in win]
        er = [br[j] * o2r[j] - bi[j] * o2i[j] for j in range(2)]
        ei = [br[j] * o2i[j] + bi[j] * o2r[j] for j in range(2)]
        pr_, pi_ = transform(er, ei, tab, False)
        mis = [pr_[j] * pr_[j] + pi_[j] * pi_[j] - inten_ref[fs[j]] for j in range(2)]
        gr, gi = transform([mis[j] * pr_[j] for j in range(2)], [mis[j] * pi_[j] for j in range(2)], tab, True)
        g2r = [br[j] * gr[j] + bi[j] * gi[j] for j in range(2)]
        g2i = [br[j] * gi[j] - bi[j] * gr[j] for j in range(2)]
        cr = [o2r[j] * gr[j] + o2i[j] * gi[j] for j in range(2)]
        ci = [o2r[j] * gi[j] - o2i[j] * gr[j] for j in range(2)]
        fr, fi = transform(cr, ci, tab, False)
        ur = [kr * fr[j] + ki * fi[j] for j in range(2)]
        ui = [kr * fi[j] - ki * fr[j] for j in range(2)]
        nr, ni = transform(ur, ui, tab, True)
        for j in range(2):
            g1r = pr[j][0] * nr[j] + pr[j][1] * ni[j]
            g1i = pr[j][0] * ni[j] - pr[j][1] * nr[j]

            @pl.when(fs[j] < count)
            def _():
                add_back(fs[j], [g1r, g1i, g2r[j], g2i[j]])
        return carry

    lax.fori_loop(0, (count + 1) // 2, pair, 0)


    if not last:
        copy = pltpu.make_async_copy(grad, outs[0], sems.at[0])
        copy.start()
        copy.wait()
    else:
        out_ref, right_ref, bottom_ref = outs
        copies = [
            pltpu.make_async_copy(grad.at[:, 3], right_ref, sems.at[9]),
            pltpu.make_async_copy(grad.at[3, pl.ds(0, 3)], bottom_ref, sems.at[10]),
        ]
        for c in copies:
            c.start()
        for rb in range(3):
            for cb in range(3):
                ext[rb, cb] = ext[rb, cb] - STEP * grad[rb, cb]
                c = pltpu.make_async_copy(
                    ext.at[rb, cb], out_ref.at[:, pl.ds(rb * B, B), pl.ds(cb * B, B)], sems.at[rb * 3 + cb]
                )
                c.start()
                copies.append(c)
        for c in copies:
            c.wait()


def frame_grads(last, positions, count, pieces, intensity, probe_field, kern, tab):
    anyspec = pl.BlockSpec(memory_space=pl.ANY)
    vmem = pl.BlockSpec(memory_space=pltpu.VMEM)
    smem = pl.BlockSpec(memory_space=pltpu.SMEM)
    shape = lambda *dims: jax.ShapeDtypeStruct(dims, jnp.float32)
    outs = [shape(4, 3 * B, 3 * B), shape(4, 4, B, B), shape(3, 4, B, B)] if last else [shape(4, 4, 4, B, B)]
    return pl.pallas_call(
        functools.partial(frames_kernel, last),
        out_shape=outs,
        in_specs=[smem, smem] + [anyspec] * len(PIECES) + [vmem] * 4,
        out_specs=[anyspec] * len(outs),
        scratch_shapes=[
            pltpu.VMEM((4, 4, 4, B, B), jnp.float32),
            pltpu.VMEM((4, 4, 4, B, B), jnp.float32),
            pltpu.SemaphoreType.DMA((16,)),
        ],
        compiler_params=pltpu.CompilerParams(vmem_limit_bytes=32 * 1024 * 1024),
        cost_estimate=pl.CostEstimate(flops=2 * 10**9, bytes_accessed=9 * 10**6, transcendentals=0),
        name="last_frames" if last else "frames",
    )(positions, count, *pieces, intensity, probe_field, kern, tab)


def passed_along(x, axis, by):
    count = lax.axis_size(axis)
    pairs = [(i, i + by) for i in range(count) if 0 <= i + by < count]
    return lax.ppermute(x, axis, pairs)


def local(object_tiles, probe_field, prop_phase, intensity, positions, counts):
    tile = object_tiles.reshape(4, 3 * B, 3 * B)

    def block(rb, cb):
        return tile[:, rb * B : (rb + 1) * B, cb * B : (cb + 1) * B]

    def blocks(places):
        return jnp.stack([block(*at) for at in places])

    places = dict(PIECES)
    count = counts[0, lax.axis_index("col")][None]
    inside = (lax.axis_index("row") < lax.axis_size("row") - 1).astype(jnp.float32)
    kern = jnp.stack([jnp.cos(prop_phase), jnp.sin(prop_phase)])
    tab = jnp.asarray(dft_tables())
    consts = (intensity, probe_field, kern, tab)

    first, top, left = blocks(places["first"]), blocks(places["top"]), blocks(places["left"])
    low = passed_along(first, "row", -1)
    bottom = passed_along(top, "row", -1)
    end_top = passed_along(first, "col", -1)
    side = passed_along(left, "col", -1)
    end_low = passed_along(low, "col", -1)
    core = blocks(places["core"])
    ends = jnp.concatenate([end_top, end_low])
    (grad,) = frame_grads(False, positions, count, (core, top, left, first, side, bottom, low, ends), *consts)

    cross = passed_along(jnp.stack([grad[0, 3], grad[3, 3]]), "col", 1)
    up = passed_along(grad[0, 1:3], "row", -1)
    down = passed_along(grad[3, 1:3], "row", 1)
    over = passed_along(grad[1:3, 3], "col", 1)
    corner_top, corner_low = grad[0, 0] + cross[0], grad[3, 0] + cross[1]
    up_first = passed_along(corner_top, "row", -1)
    down_first = passed_along(corner_low, "row", 1)
    g_left = grad[1:3, 0] + over
    g_side = passed_along(g_left, "col", -1)
    g_first = corner_top + down_first
    g_low = (corner_low + up_first) * inside
    g_ends = passed_along(jnp.stack([g_first, g_low]), "col", -1)

    core = core - STEP * grad[1:3, 1:3].reshape(core.shape)
    top = top - STEP * (grad[0, 1:3] + down)
    left = left - STEP * g_left
    first = first - STEP * g_first[None]
    side = side - STEP * g_side
    bottom = bottom - STEP * ((grad[3, 1:3] + up) * inside)
    low = low - STEP * g_low[None]
    ends = ends - STEP * g_ends
    out, right, under = frame_grads(True, positions, count, (core, top, left, first, side, bottom, low, ends), *consts)

    cross = passed_along(right[3], "col", 1)
    down = passed_along(under[1:3], "row", 1)
    over = passed_along(right[0:3], "col", 1)
    down_first = passed_along(under[0] + cross, "row", 1)
    top_add = jnp.concatenate([down_first, down[0], down[1]], axis=2)
    left_add = over.transpose(1, 0, 2, 3).reshape(4, 3 * B, B)
    out = out.at[:, :B, :].add(-STEP * top_add)
    out = out.at[:, :, :B].add(-STEP * left_add)
    return out.reshape(object_tiles.shape)


def solution(mesh):
    return jax.shard_map(
        local,
        mesh=mesh,
        in_specs=(
            P(None, None, "row", "col"),
            P(),
            P(),
            P(("row", "col"), None, None),
            P(("row", "col"), None),
            P("row", None),
        ),
        out_specs=P(None, None, "row", "col"),
        check_vma=False,
    )
```

```python
import functools

import numpy as np
import jax
import jax.numpy as jnp
from jax import lax
from jax.experimental import pallas as pl
from jax.experimental.pallas import tpu as pltpu
from jax.sharding import PartitionSpec as P
import ml_dtypes

ITERS = 2
STEP = 0.2
B = 128
ROWS, RING = 16, 4
SHARE = 32
GROUP = 8


def dft_tables():
    k = np.arange(B)
    phase = (np.outer(k, k) % B) * (2.0 * np.pi / B)
    c, s = np.cos(phase) / np.sqrt(B), -np.sin(phase) / np.sqrt(B)
    forward = np.block([[c, s], [-s, c]]).astype(np.float32)
    parts = []
    for full in (forward, forward.T):
        high = full.astype(ml_dtypes.bfloat16)
        low = (full - high.astype(np.float32)).astype(ml_dtypes.bfloat16)
        parts += [high, low]
    return np.stack(parts)


def split(x):
    high = x.astype(jnp.bfloat16)
    low = (x - high.astype(jnp.float32)).astype(jnp.bfloat16)
    return high, low


def dot(a, b):
    return jnp.dot(a, b, preferred_element_type=jnp.float32)


def right_mul(x, tab, at):
    high, low = split(x)
    t_high, t_low = tab[at], tab[at + 1]
    return dot(high, t_high) + (dot(low, t_high) + dot(high, t_low))


def left_mul(x, tab, at):
    high, low = split(x)
    t_high, t_low = tab[at], tab[at + 1]
    return dot(t_high, high) + (dot(t_high, low) + dot(t_low, high))


def transform(re, im, tab, inverse):
    first, second = (2, 0) if inverse else (0, 2)
    count = len(re)
    x = jnp.concatenate([jnp.concatenate([r, i], axis=1) for r, i in zip(re, im)], axis=0)
    y = right_mul(x, tab, first)
    y = [y[j * B : (j + 1) * B] for j in range(count)]
    y = jnp.concatenate(
        [jnp.concatenate([v[:, :B] for v in y], axis=1), jnp.concatenate([v[:, B:] for v in y], axis=1)], axis=0
    )
    z = left_mul(y, tab, second)
    return [z[:B, j * B : (j + 1) * B] for j in range(count)], [z[B:, j * B : (j + 1) * B] for j in range(count)]


PIECES = (
    ("core", ((1, 1), (1, 2), (2, 1), (2, 2))),
    ("top", ((0, 1), (0, 2))),
    ("left", ((1, 0), (2, 0))),
    ("first", ((0, 0),)),
    ("side", ((1, 3), (2, 3))),
    ("bottom", ((3, 1), (3, 2))),
    ("low", ((3, 0),)),
    ("ends", ((0, 3), (3, 3))),
)


def whole_blocks(ext, tile, right, low, bottom, rest, corner):
    for rb in range(3):
        for cb in range(3):
            yield tile.at[:, pl.ds(rb * B, B), pl.ds(cb * B, B)], ext.at[rb, cb]
        yield right.at[:, pl.ds(rb * B, B), :], ext.at[rb, 3]
    yield low, ext.at[3, 0]
    for cb in (1, 2):
        cols = pl.ds((cb - 1) * B, B)
        yield bottom.at[:, :, cols], ext.at[3, cb, :, pl.ds(0, B - SHARE), :]
        yield rest.at[:, :, cols], ext.at[3, cb, :, pl.ds(B - SHARE, SHARE), :]
    yield corner, ext.at[3, 3]


def piece_blocks(ext, *pieces):
    for ref, (_, places) in zip(pieces, PIECES):
        for number, (rb, cb) in enumerate(places):
            yield ref.at[number], ext.at[rb, cb]


def frames_kernel(last, n_pieces, pos_ref, cnt_ref, *refs):
    pieces, refs = refs[:n_pieces], refs[n_pieces:]
    inten_from, probe_ref, kern_ref, tab_from = refs[:4]
    outs, (ext, grad, inten_ref, tab, sems, late_sem) = refs[4:-6], refs[-6:]
    late = pltpu.make_async_copy(inten_from, inten_ref, late_sem)
    copies = [pltpu.make_async_copy(tab_from, tab, sems.at[0])]
    for src, dst in (piece_blocks if last else whole_blocks)(ext, *pieces):
        copies.append(pltpu.make_async_copy(src, dst, sems.at[len(copies)]))
    for c in copies:
        c.start()
    late.start()
    grad[...] = jnp.zeros_like(grad)
    for c in copies:
        c.wait()
    rows = lax.broadcasted_iota(jnp.int32, (B, B), 0)
    cols = lax.broadcasted_iota(jnp.int32, (B, B), 1)
    count = cnt_ref[0]

    def where_is(f):
        t, l = pos_ref[f, 0], pos_ref[f, 1]
        return t // B, lax.rem(t, B), l // B, lax.rem(l, B)

    def window(f):
        tb, ts, lb, ls = where_is(f)
        rm, cm = rows >= ts, cols >= ls

        def plane(k):
            upper = jnp.where(cm, ext[tb, lb, k], ext[tb, lb + 1, k])
            lower = jnp.where(cm, ext[tb + 1, lb, k], ext[tb + 1, lb + 1, k])
            return jnp.where(rm, upper, lower)

        return plane

    def probe(f):
        tb, ts, lb, ls = where_is(f)
        return [pltpu.roll(pltpu.roll(probe_ref[k], ts, 0), ls, 1) for k in range(2)]

    def add_back(f, planes):
        tb, ts, lb, ls = where_is(f)
        rm, cm = rows >= ts, cols >= ls
        zero = jnp.zeros((B, B), jnp.float32)
        for k, g in enumerate(planes):
            upper = jnp.where(rm, g, zero)
            lower = g - upper
            for db, part in ((0, upper), (1, lower)):
                left = jnp.where(cm, part, zero)
                grad[tb + db, lb, k] += left
                grad[tb + db, lb + 1, k] += part - left

    def group(p, carry):
        fs = [GROUP * p + j for j in range(GROUP)]
        win = [window(f) for f in fs]
        pr = [probe(f) for f in fs]
        o1r, o1i = [w(0) for w in win], [w(1) for w in win]
        ar = [pr[j][0] * o1r[j] - pr[j][1] * o1i[j] for j in range(GROUP)]
        ai = [pr[j][0] * o1i[j] + pr[j][1] * o1r[j] for j in range(GROUP)]
        fr, fi = transform(ar, ai, tab, False)
        kr, ki = kern_ref[0], kern_ref[1]
        mr = [kr * fr[j] - ki * fi[j] for j in range(GROUP)]
        mi = [kr * fi[j] + ki * fr[j] for j in range(GROUP)]
        br, bi = transform(mr, mi, tab, True)
        o2r, o2i = [w(2) for w in win], [w(3) for w in win]
        er = [br[j] * o2r[j] - bi[j] * o2i[j] for j in range(GROUP)]
        ei = [br[j] * o2i[j] + bi[j] * o2r[j] for j in range(GROUP)]
        pr_, pi_ = transform(er, ei, tab, False)
        late.wait()
        mis = [pr_[j] * pr_[j] + pi_[j] * pi_[j] - inten_ref[fs[j]] for j in range(GROUP)]
        gr, gi = transform([mis[j] * pr_[j] for j in range(GROUP)], [mis[j] * pi_[j] for j in range(GROUP)], tab, True)
        g2r = [br[j] * gr[j] + bi[j] * gi[j] for j in range(GROUP)]
        g2i = [br[j] * gi[j] - bi[j] * gr[j] for j in range(GROUP)]
        cr = [o2r[j] * gr[j] + o2i[j] * gi[j] for j in range(GROUP)]
        ci = [o2r[j] * gi[j] - o2i[j] * gr[j] for j in range(GROUP)]
        fr, fi = transform(cr, ci, tab, False)
        ur = [kr * fr[j] + ki * fi[j] for j in range(GROUP)]
        ui = [kr * fi[j] - ki * fr[j] for j in range(GROUP)]
        nr, ni = transform(ur, ui, tab, True)
        for j in range(GROUP):
            g1r = pr[j][0] * nr[j] + pr[j][1] * ni[j]
            g1i = pr[j][0] * ni[j] - pr[j][1] * nr[j]

            @pl.when(fs[j] < count)
            def _():
                add_back(fs[j], [g1r, g1i, g2r[j], g2i[j]])
        return carry

    group(0, 0)


    if not last:
        copies = [pltpu.make_async_copy(grad, outs[0], sems.at[0])]
        copies[0].start()
        for rb in range(4):
            for cb in range(3):
                ext[rb, cb] = ext[rb, cb] - STEP * grad[rb, cb]
            c = pltpu.make_async_copy(ext.at[rb, pl.ds(0, 3)], outs[1].at[rb], sems.at[1 + rb])
            c.start()
            copies.append(c)
    else:
        out_ref, right_ref, bottom_ref = outs
        copies = [
            pltpu.make_async_copy(grad.at[:, 3], right_ref, sems.at[9]),
            pltpu.make_async_copy(grad.at[3, pl.ds(0, 3)], bottom_ref, sems.at[10]),
        ]
        for c in copies:
            c.start()
        for rb in range(3):
            for cb in range(3):
                ext[rb, cb] = ext[rb, cb] - STEP * grad[rb, cb]
                c = pltpu.make_async_copy(
                    ext.at[rb, cb], out_ref.at[:, pl.ds(rb * B, B), pl.ds(cb * B, B)], sems.at[rb * 3 + cb]
                )
                c.start()
                copies.append(c)
    for c in copies:
        c.wait()


def frame_grads(last, positions, count, pieces, intensity, probe_field, kern, tab):
    anyspec = pl.BlockSpec(memory_space=pl.ANY)
    vmem = pl.BlockSpec(memory_space=pltpu.VMEM)
    hbm = pl.BlockSpec(memory_space=pltpu.HBM)
    smem = pl.BlockSpec(memory_space=pltpu.SMEM)
    shape = lambda *dims: jax.ShapeDtypeStruct(dims, jnp.float32)
    if last:
        outs = [shape(4, 3 * B, 3 * B), shape(4, 4, B, B), shape(3, 4, B, B)]
    else:
        outs = [shape(4, 4, 4, B, B), shape(4, 3, 4, B, B)]
    return pl.pallas_call(
        functools.partial(frames_kernel, last, len(pieces)),
        out_shape=outs,
        in_specs=[smem, smem] + [anyspec if last else hbm] * len(pieces) + [hbm, vmem, vmem, hbm],
        out_specs=[anyspec] * len(outs),
        scratch_shapes=[
            pltpu.VMEM((4, 4, 4, B, B), jnp.float32),
            pltpu.VMEM((4, 4, 4, B, B), jnp.float32),
            pltpu.VMEM((8, B, B), jnp.float32),
            pltpu.VMEM((4, 2 * B, 2 * B), jnp.bfloat16),
            pltpu.SemaphoreType.DMA((24,)),
            pltpu.SemaphoreType.DMA,
        ],
        compiler_params=pltpu.CompilerParams(vmem_limit_bytes=(32 if last else 60) * 1024 * 1024),
        cost_estimate=pl.CostEstimate(flops=2 * 10**9, bytes_accessed=9 * 10**6, transcendentals=0),
        name="last_frames" if last else "frames",
    )(positions, count, *pieces, intensity, probe_field, kern, tab)


def passed_around(x, by):
    places = [(y, z) for y in range(ROWS // RING) for z in range(RING)]
    for step in range(RING - 1):
        pairs = []
        for y, z in places:
            z_to = (z - by) % RING
            y_to = y
            if step == RING - 2:
                start = (z + by * step) % RING
                y_to = y + (start + by) // RING
            if 0 <= y_to < ROWS // RING:
                pairs.append((y * RING + z, y_to * RING + z_to))
        x = lax.ppermute(x, "row", pairs)
    return x


def passed_along(x, axis, by):
    count = lax.axis_size(axis)
    pairs = [(i, i + by) for i in range(count) if 0 <= i + by < count]
    return lax.ppermute(x, axis, pairs)


def local(object_tiles, probe_field, prop_phase, intensity, positions, counts):
    tile = object_tiles.reshape(4, 3 * B, 3 * B)
    count = counts[0, lax.axis_index("col")][None]
    inside = (lax.axis_index("row") < lax.axis_size("row") - 1).astype(jnp.float32)
    kern = jnp.stack([jnp.cos(prop_phase), jnp.sin(prop_phase)])
    tab = jnp.asarray(dft_tables())
    consts = (intensity, probe_field, kern, tab)

    low = passed_along(tile[:, :B, :B], "row", -1)
    bottom = passed_along(tile[:, : B - SHARE, B:], "row", -1)
    rest = passed_around(tile[:, B - SHARE : B, B:], -1)
    right = passed_along(tile[:, :, :B], "col", -1)
    corner = passed_along(low, "col", -1)
    grad, moved = frame_grads(
        False, positions, count, (tile, right, low, bottom, rest, corner), *consts
    )

    cross = passed_along(jnp.stack([grad[0, 3], grad[3, 3]]), "col", 1)
    up = passed_along(grad[0, 1:3], "row", -1)
    down = passed_along(grad[3, 1:3], "row", 1)
    over = passed_along(grad[1:3, 3], "col", 1)
    up_first = passed_along(grad[0, 0] + cross[0], "row", -1)
    down_first = passed_along(grad[3, 0] + cross[1], "row", 1)
    left = moved[1:3, 0] - STEP * over
    side = passed_along(left, "col", -1)
    first = moved[0, 0] - STEP * (cross[0] + down_first)
    low = (moved[3, 0] - STEP * (cross[1] + up_first)) * inside
    ends = passed_along(jnp.stack([first, low]), "col", -1)
    core = moved[1:3, 1:3].reshape(4, 4, B, B)
    top = moved[0, 1:3] - STEP * down
    bottom = (moved[3, 1:3] - STEP * up) * inside
    pieces = (core, top, left, first[None], side, bottom, low[None], ends)
    out, right, under = frame_grads(True, positions, count, pieces, *consts)

    cross = passed_along(right[3], "col", 1)
    down = passed_along(under[1:3, :, : B - SHARE], "row", 1)
    rest = passed_around(under[1:3, :, B - SHARE :], 1)
    down = jnp.concatenate([down, rest], axis=2)
    over = passed_along(right[0:3], "col", 1)
    down_first = passed_along(under[0] + cross, "row", 1)
    top_add = jnp.concatenate([down_first, down[0], down[1]], axis=2)
    left_add = over.transpose(1, 0, 2, 3).reshape(4, 3 * B, B)
    out = out.at[:, :B, :].add(-STEP * top_add)
    out = out.at[:, :, :B].add(-STEP * left_add)
    return out.reshape(object_tiles.shape)


def solution(mesh):
    return jax.shard_map(
        local,
        mesh=mesh,
        in_specs=(
            P(None, None, "row", "col"),
            P(),
            P(),
            P(("row", "col"), None, None),
            P(("row", "col"), None),
            P("row", None),
        ),
        out_specs=P(None, None, "row", "col"),
        check_vma=False,
    )
```

```python
import functools

import numpy as np
import jax
import jax.numpy as jnp
from jax import lax
from jax.experimental import pallas as pl
from jax.experimental.pallas import tpu as pltpu
from jax.sharding import PartitionSpec as P
import ml_dtypes

ITERS = 2
STEP = 0.2
B = 128
ROWS, RING = 16, 4
SHARE = 32
GROUP = 8


def dft_tables():
    k = np.arange(B)
    phase = (np.outer(k, k) % B) * (2.0 * np.pi / B)
    c, s = np.cos(phase) / np.sqrt(B), -np.sin(phase) / np.sqrt(B)
    forward = np.block([[c, s], [-s, c]]).astype(np.float32)
    parts = []
    for full in (forward, forward.T):
        high = full.astype(ml_dtypes.bfloat16)
        low = (full - high.astype(np.float32)).astype(ml_dtypes.bfloat16)
        parts += [high, low]
    return np.stack(parts)


def split(x):
    high = x.astype(jnp.bfloat16)
    low = (x - high.astype(jnp.float32)).astype(jnp.bfloat16)
    return high, low


def dot(a, b):
    return jnp.dot(a, b, preferred_element_type=jnp.float32)


def right_mul(x, tab, at):
    high, low = split(x)
    t_high, t_low = tab[at], tab[at + 1]
    return dot(high, t_high) + (dot(low, t_high) + dot(high, t_low))


def left_mul(x, tab, at):
    high, low = split(x)
    t_high, t_low = tab[at], tab[at + 1]
    return dot(t_high, high) + (dot(t_high, low) + dot(t_low, high))


def transform(re, im, tab, inverse):
    first, second = (2, 0) if inverse else (0, 2)
    count = len(re)
    x = jnp.concatenate([jnp.concatenate([r, i], axis=1) for r, i in zip(re, im)], axis=0)
    y = right_mul(x, tab, first)
    y = [y[j * B : (j + 1) * B] for j in range(count)]
    y = jnp.concatenate(
        [jnp.concatenate([v[:, :B] for v in y], axis=1), jnp.concatenate([v[:, B:] for v in y], axis=1)], axis=0
    )
    z = left_mul(y, tab, second)
    return [z[:B, j * B : (j + 1) * B] for j in range(count)], [z[B:, j * B : (j + 1) * B] for j in range(count)]


PIECES = (
    ("core", ((1, 1), (1, 2), (2, 1), (2, 2))),
    ("top", ((0, 1), (0, 2))),
    ("left", ((1, 0), (2, 0))),
    ("first", ((0, 0),)),
    ("side", ((1, 3), (2, 3))),
    ("bottom", ((3, 1), (3, 2))),
    ("low", ((3, 0),)),
    ("ends", ((0, 3), (3, 3))),
)


def whole_blocks(ext, tile, right, low, bottom, rest, corner):
    for rb in range(3):
        for cb in range(3):
            yield tile.at[:, pl.ds(rb * B, B), pl.ds(cb * B, B)], ext.at[rb, cb]
        yield right.at[:, pl.ds(rb * B, B), :], ext.at[rb, 3]
    yield low, ext.at[3, 0]
    for cb in (1, 2):
        cols = pl.ds((cb - 1) * B, B)
        yield bottom.at[:, :, cols], ext.at[3, cb, :, pl.ds(0, B - SHARE), :]
        yield rest.at[:, :, cols], ext.at[3, cb, :, pl.ds(B - SHARE, SHARE), :]
    yield corner, ext.at[3, 3]


def piece_blocks(ext, *pieces):
    for ref, (_, places) in zip(pieces, PIECES):
        for number, (rb, cb) in enumerate(places):
            yield ref.at[number], ext.at[rb, cb]


def frames_kernel(last, n_pieces, pos_ref, cnt_ref, *refs):
    pieces, refs = refs[:n_pieces], refs[n_pieces:]
    inten_from, probe_ref, kern_ref, tab_from = refs[:4]
    outs, (ext, grad, inten_ref, tab, sems, late_sem) = refs[4:-6], refs[-6:]
    late = pltpu.make_async_copy(inten_from, inten_ref, late_sem)
    copies = [pltpu.make_async_copy(tab_from, tab, sems.at[0])]
    for src, dst in (piece_blocks if last else whole_blocks)(ext, *pieces):
        copies.append(pltpu.make_async_copy(src, dst, sems.at[len(copies)]))
    for c in copies:
        c.start()
    late.start()
    grad[...] = jnp.zeros_like(grad)
    for c in copies:
        c.wait()
    rows = lax.broadcasted_iota(jnp.int32, (B, B), 0)
    cols = lax.broadcasted_iota(jnp.int32, (B, B), 1)
    count = cnt_ref[0]

    def where_is(f):
        t, l = pos_ref[f, 0], pos_ref[f, 1]
        return t // B, lax.rem(t, B), l // B, lax.rem(l, B)

    def window(f):
        tb, ts, lb, ls = where_is(f)
        rm, cm = rows >= ts, cols >= ls

        def plane(k):
            upper = jnp.where(cm, ext[tb, lb, k], ext[tb, lb + 1, k])
            lower = jnp.where(cm, ext[tb + 1, lb, k], ext[tb + 1, lb + 1, k])
            return jnp.where(rm, upper, lower)

        return plane

    def probe(f):
        tb, ts, lb, ls = where_is(f)
        return [pltpu.roll(pltpu.roll(probe_ref[k], ts, 0), ls, 1) for k in range(2)]

    def add_back(f, planes):
        tb, ts, lb, ls = where_is(f)
        rm, cm = rows >= ts, cols >= ls
        zero = jnp.zeros((B, B), jnp.float32)
        for k, g in enumerate(planes):
            upper = jnp.where(rm, g, zero)
            lower = g - upper
            for db, part in ((0, upper), (1, lower)):
                left = jnp.where(cm, part, zero)
                grad[tb + db, lb, k] += left
                grad[tb + db, lb + 1, k] += part - left

    def group(p, carry):
        fs = [GROUP * p + j for j in range(GROUP)]
        win = [window(f) for f in fs]
        pr = [probe(f) for f in fs]
        o1r, o1i = [w(0) for w in win], [w(1) for w in win]
        ar = [pr[j][0] * o1r[j] - pr[j][1] * o1i[j] for j in range(GROUP)]
        ai = [pr[j][0] * o1i[j] + pr[j][1] * o1r[j] for j in range(GROUP)]
        fr, fi = transform(ar, ai, tab, False)
        kr, ki = kern_ref[0], kern_ref[1]
        mr = [kr * fr[j] - ki * fi[j] for j in range(GROUP)]
        mi = [kr * fi[j] + ki * fr[j] for j in range(GROUP)]
        br, bi = transform(mr, mi, tab, True)
        o2r, o2i = [w(2) for w in win], [w(3) for w in win]
        er = [br[j] * o2r[j] - bi[j] * o2i[j] for j in range(GROUP)]
        ei = [br[j] * o2i[j] + bi[j] * o2r[j] for j in range(GROUP)]
        pr_, pi_ = transform(er, ei, tab, False)
        late.wait()
        mis = [pr_[j] * pr_[j] + pi_[j] * pi_[j] - inten_ref[fs[j]] for j in range(GROUP)]
        gr, gi = transform([mis[j] * pr_[j] for j in range(GROUP)], [mis[j] * pi_[j] for j in range(GROUP)], tab, True)
        g2r = [br[j] * gr[j] + bi[j] * gi[j] for j in range(GROUP)]
        g2i = [br[j] * gi[j] - bi[j] * gr[j] for j in range(GROUP)]
        cr = [o2r[j] * gr[j] + o2i[j] * gi[j] for j in range(GROUP)]
        ci = [o2r[j] * gi[j] - o2i[j] * gr[j] for j in range(GROUP)]
        fr, fi = transform(cr, ci, tab, False)
        ur = [kr * fr[j] + ki * fi[j] for j in range(GROUP)]
        ui = [kr * fi[j] - ki * fr[j] for j in range(GROUP)]
        nr, ni = transform(ur, ui, tab, True)
        for j in range(GROUP):
            g1r = pr[j][0] * nr[j] + pr[j][1] * ni[j]
            g1i = pr[j][0] * ni[j] - pr[j][1] * nr[j]

            @pl.when(fs[j] < count)
            def _():
                add_back(fs[j], [g1r, g1i, g2r[j], g2i[j]])
        return carry

    group(0, 0)


    if not last:
        copies = [pltpu.make_async_copy(grad, outs[0], sems.at[0])]
        copies[0].start()
        for rb in range(4):
            for cb in range(3):
                ext[rb, cb] = ext[rb, cb] - STEP * grad[rb, cb]
            c = pltpu.make_async_copy(ext.at[rb, pl.ds(0, 3)], outs[1].at[rb], sems.at[1 + rb])
            c.start()
            copies.append(c)
    else:
        out_ref, right_ref, bottom_ref = outs
        copies = [
            pltpu.make_async_copy(grad.at[:, 3], right_ref, sems.at[9]),
            pltpu.make_async_copy(grad.at[3, pl.ds(0, 3)], bottom_ref, sems.at[10]),
        ]
        for c in copies:
            c.start()
        for rb in range(3):
            for cb in range(3):
                ext[rb, cb] = ext[rb, cb] - STEP * grad[rb, cb]
                c = pltpu.make_async_copy(
                    ext.at[rb, cb], out_ref.at[:, pl.ds(rb * B, B), pl.ds(cb * B, B)], sems.at[rb * 3 + cb]
                )
                c.start()
                copies.append(c)
    for c in copies:
        c.wait()


def frame_grads(last, positions, count, pieces, intensity, probe_field, kern, tab):
    anyspec = pl.BlockSpec(memory_space=pl.ANY)
    vmem = pl.BlockSpec(memory_space=pltpu.VMEM)
    hbm = pl.BlockSpec(memory_space=pltpu.HBM)
    smem = pl.BlockSpec(memory_space=pltpu.SMEM)
    shape = lambda *dims: jax.ShapeDtypeStruct(dims, jnp.float32)
    if last:
        outs = [shape(4, 3 * B, 3 * B), shape(4, 4, B, B), shape(3, 4, B, B)]
    else:
        outs = [shape(4, 4, 4, B, B), shape(4, 3, 4, B, B)]
    return pl.pallas_call(
        functools.partial(frames_kernel, last, len(pieces)),
        out_shape=outs,
        in_specs=[smem, smem] + [anyspec if last else hbm] * len(pieces) + [hbm, vmem, vmem, hbm],
        out_specs=[anyspec] * len(outs),
        scratch_shapes=[
            pltpu.VMEM((4, 4, 4, B, B), jnp.float32),
            pltpu.VMEM((4, 4, 4, B, B), jnp.float32),
            pltpu.VMEM((8, B, B), jnp.float32),
            pltpu.VMEM((4, 2 * B, 2 * B), jnp.bfloat16),
            pltpu.SemaphoreType.DMA((24,)),
            pltpu.SemaphoreType.DMA,
        ],
        compiler_params=pltpu.CompilerParams(vmem_limit_bytes=(32 if last else 50) * 1024 * 1024),
        cost_estimate=pl.CostEstimate(flops=2 * 10**9, bytes_accessed=9 * 10**6, transcendentals=0),
        name="last_frames" if last else "frames",
    )(positions, count, *pieces, intensity, probe_field, kern, tab)


def passed_around(x, by):
    places = [(y, z) for y in range(ROWS // RING) for z in range(RING)]
    for step in range(RING - 1):
        pairs = []
        for y, z in places:
            z_to = (z - by) % RING
            y_to = y
            if step == RING - 2:
                start = (z + by * step) % RING
                y_to = y + (start + by) // RING
            if 0 <= y_to < ROWS // RING:
                pairs.append((y * RING + z, y_to * RING + z_to))
        x = lax.ppermute(x, "row", pairs)
    return x


def passed_along(x, axis, by):
    count = lax.axis_size(axis)
    pairs = [(i, i + by) for i in range(count) if 0 <= i + by < count]
    return lax.ppermute(x, axis, pairs)


def local(object_tiles, probe_field, prop_phase, intensity, positions, counts):
    tile = object_tiles.reshape(4, 3 * B, 3 * B)
    count = counts[0, lax.axis_index("col")][None]
    inside = (lax.axis_index("row") < lax.axis_size("row") - 1).astype(jnp.float32)
    kern = jnp.stack([jnp.cos(prop_phase), jnp.sin(prop_phase)])
    tab = jnp.asarray(dft_tables())
    consts = (intensity, probe_field, kern, tab)

    low = passed_along(tile[:, :B, :B], "row", -1)
    bottom = passed_along(tile[:, : B - SHARE, B:], "row", -1)
    rest = passed_around(tile[:, B - SHARE : B, B:], -1)
    right = passed_along(tile[:, :, :B], "col", -1)
    corner = passed_along(low, "col", -1)
    grad, moved = frame_grads(
        False, positions, count, (tile, right, low, bottom, rest, corner), *consts
    )

    cross = passed_along(jnp.stack([grad[0, 3], grad[3, 3]]), "col", 1)
    up = passed_along(grad[0, 1:3], "row", -1)
    down = passed_along(grad[3, 1:3], "row", 1)
    over = passed_along(grad[1:3, 3], "col", 1)
    up_first = passed_along(grad[0, 0] + cross[0], "row", -1)
    down_first = passed_along(grad[3, 0] + cross[1], "row", 1)
    left = moved[1:3, 0] - STEP * over
    side = passed_along(left, "col", -1)
    first = moved[0, 0] - STEP * (cross[0] + down_first)
    low = (moved[3, 0] - STEP * (cross[1] + up_first)) * inside
    ends = passed_along(jnp.stack([first, low]), "col", -1)
    core = moved[1:3, 1:3].reshape(4, 4, B, B)
    top = moved[0, 1:3] - STEP * down
    bottom = (moved[3, 1:3] - STEP * up) * inside
    pieces = (core, top, left, first[None], side, bottom, low[None], ends)
    out, right, under = frame_grads(True, positions, count, pieces, *consts)

    cross = passed_along(right[3], "col", 1)
    down = passed_along(under[1:3, :, : B - SHARE], "row", 1)
    rest = passed_around(under[1:3, :, B - SHARE :], 1)
    down = jnp.concatenate([down, rest], axis=2)
    over = passed_along(right[0:3], "col", 1)
    down_first = passed_along(under[0] + cross, "row", 1)
    top_add = jnp.concatenate([down_first, down[0], down[1]], axis=2)
    left_add = over.transpose(1, 0, 2, 3).reshape(4, 3 * B, B)
    out = out.at[:, :B, :].add(-STEP * top_add)
    out = out.at[:, :, :B].add(-STEP * left_add)
    return out.reshape(object_tiles.shape)


def solution(mesh):
    return jax.shard_map(
        local,
        mesh=mesh,
        in_specs=(
            P(None, None, "row", "col"),
            P(),
            P(),
            P(("row", "col"), None, None),
            P(("row", "col"), None),
            P("row", None),
        ),
        out_specs=P(None, None, "row", "col"),
        check_vma=False,
    )
```

```python
import functools

import numpy as np
import jax
import jax.numpy as jnp
from jax import lax
from jax.experimental import pallas as pl
from jax.experimental.pallas import tpu as pltpu
from jax.sharding import PartitionSpec as P
import ml_dtypes

ITERS = 2
STEP = 0.2
B = 128
ROWS, RING = 16, 4
SHARE = 24
GROUP = 8


def dft_tables():
    k = np.arange(B)
    phase = (np.outer(k, k) % B) * (2.0 * np.pi / B)
    c, s = np.cos(phase) / np.sqrt(B), -np.sin(phase) / np.sqrt(B)
    forward = np.block([[c, s], [-s, c]]).astype(np.float32)
    parts = []
    for full in (forward, forward.T):
        high = full.astype(ml_dtypes.bfloat16)
        low = (full - high.astype(np.float32)).astype(ml_dtypes.bfloat16)
        parts += [high, low]
    return np.stack(parts)


def split(x):
    high = x.astype(jnp.bfloat16)
    low = (x - high.astype(jnp.float32)).astype(jnp.bfloat16)
    return high, low


def dot(a, b):
    return jnp.dot(a, b, preferred_element_type=jnp.float32)


def right_mul(x, tab, at):
    high, low = split(x)
    t_high, t_low = tab[at], tab[at + 1]
    return dot(high, t_high) + (dot(low, t_high) + dot(high, t_low))


def left_mul(x, tab, at):
    high, low = split(x)
    t_high, t_low = tab[at], tab[at + 1]
    return dot(t_high, high) + (dot(t_high, low) + dot(t_low, high))


def transform(re, im, tab, inverse):
    first, second = (2, 0) if inverse else (0, 2)
    count = len(re)
    x = jnp.concatenate([jnp.concatenate([r, i], axis=1) for r, i in zip(re, im)], axis=0)
    y = right_mul(x, tab, first)
    y = [y[j * B : (j + 1) * B] for j in range(count)]
    y = jnp.concatenate(
        [jnp.concatenate([v[:, :B] for v in y], axis=1), jnp.concatenate([v[:, B:] for v in y], axis=1)], axis=0
    )
    z = left_mul(y, tab, second)
    return [z[:B, j * B : (j + 1) * B] for j in range(count)], [z[B:, j * B : (j + 1) * B] for j in range(count)]


PIECES = (
    ("core", ((1, 1), (1, 2), (2, 1), (2, 2))),
    ("top", ((0, 1), (0, 2))),
    ("left", ((1, 0), (2, 0))),
    ("first", ((0, 0),)),
    ("side", ((1, 3), (2, 3))),
    ("bottom", ((3, 1), (3, 2))),
    ("low", ((3, 0),)),
    ("ends", ((0, 3), (3, 3))),
)


def whole_blocks(ext, tile, right, low, bottom, rest, corner):
    for rb in range(3):
        for cb in range(3):
            yield tile.at[:, pl.ds(rb * B, B), pl.ds(cb * B, B)], ext.at[rb, cb]
        yield right.at[:, pl.ds(rb * B, B), :], ext.at[rb, 3]
    yield low, ext.at[3, 0]
    for cb in (1, 2):
        cols = pl.ds((cb - 1) * B, B)
        yield bottom.at[:, :, cols], ext.at[3, cb, :, pl.ds(0, B - SHARE), :]
        yield rest.at[:, :, cols], ext.at[3, cb, :, pl.ds(B - SHARE, SHARE), :]
    yield corner, ext.at[3, 3]


def piece_blocks(ext, *pieces):
    for ref, (_, places) in zip(pieces, PIECES):
        for number, (rb, cb) in enumerate(places):
            yield ref.at[number], ext.at[rb, cb]


def frames_kernel(last, n_pieces, pos_ref, cnt_ref, *refs):
    pieces, refs = refs[:n_pieces], refs[n_pieces:]
    inten_from, probe_ref, kern_ref, tab_from = refs[:4]
    outs, (ext, grad, inten_ref, tab, sems, late_sem) = refs[4:-6], refs[-6:]
    late = pltpu.make_async_copy(inten_from, inten_ref, late_sem)
    copies = [pltpu.make_async_copy(tab_from, tab, sems.at[0])]
    for src, dst in (piece_blocks if last else whole_blocks)(ext, *pieces):
        copies.append(pltpu.make_async_copy(src, dst, sems.at[len(copies)]))
    for c in copies:
        c.start()
    late.start()
    grad[...] = jnp.zeros_like(grad)
    for c in copies:
        c.wait()
    rows = lax.broadcasted_iota(jnp.int32, (B, B), 0)
    cols = lax.broadcasted_iota(jnp.int32, (B, B), 1)
    count = cnt_ref[0]

    def where_is(f):
        t, l = pos_ref[f, 0], pos_ref[f, 1]
        return t // B, lax.rem(t, B), l // B, lax.rem(l, B)

    def window(f):
        tb, ts, lb, ls = where_is(f)
        rm, cm = rows >= ts, cols >= ls

        def plane(k):
            upper = jnp.where(cm, ext[tb, lb, k], ext[tb, lb + 1, k])
            lower = jnp.where(cm, ext[tb + 1, lb, k], ext[tb + 1, lb + 1, k])
            return jnp.where(rm, upper, lower)

        return plane

    def probe(f):
        tb, ts, lb, ls = where_is(f)
        return [pltpu.roll(pltpu.roll(probe_ref[k], ts, 0), ls, 1) for k in range(2)]

    def add_back(f, planes):
        tb, ts, lb, ls = where_is(f)
        rm, cm = rows >= ts, cols >= ls
        zero = jnp.zeros((B, B), jnp.float32)
        for k, g in enumerate(planes):
            upper = jnp.where(rm, g, zero)
            lower = g - upper
            for db, part in ((0, upper), (1, lower)):
                left = jnp.where(cm, part, zero)
                grad[tb + db, lb, k] += left
                grad[tb + db, lb + 1, k] += part - left

    def group(p, carry):
        fs = [GROUP * p + j for j in range(GROUP)]
        win = [window(f) for f in fs]
        pr = [probe(f) for f in fs]
        o1r, o1i = [w(0) for w in win], [w(1) for w in win]
        ar = [pr[j][0] * o1r[j] - pr[j][1] * o1i[j] for j in range(GROUP)]
        ai = [pr[j][0] * o1i[j] + pr[j][1] * o1r[j] for j in range(GROUP)]
        fr, fi = transform(ar, ai, tab, False)
        kr, ki = kern_ref[0], kern_ref[1]
        mr = [kr * fr[j] - ki * fi[j] for j in range(GROUP)]
        mi = [kr * fi[j] + ki * fr[j] for j in range(GROUP)]
        br, bi = transform(mr, mi, tab, True)
        o2r, o2i = [w(2) for w in win], [w(3) for w in win]
        er = [br[j] * o2r[j] - bi[j] * o2i[j] for j in range(GROUP)]
        ei = [br[j] * o2i[j] + bi[j] * o2r[j] for j in range(GROUP)]
        pr_, pi_ = transform(er, ei, tab, False)
        late.wait()
        mis = [pr_[j] * pr_[j] + pi_[j] * pi_[j] - inten_ref[fs[j]] for j in range(GROUP)]
        gr, gi = transform([mis[j] * pr_[j] for j in range(GROUP)], [mis[j] * pi_[j] for j in range(GROUP)], tab, True)
        g2r = [br[j] * gr[j] + bi[j] * gi[j] for j in range(GROUP)]
        g2i = [br[j] * gi[j] - bi[j] * gr[j] for j in range(GROUP)]
        cr = [o2r[j] * gr[j] + o2i[j] * gi[j] for j in range(GROUP)]
        ci = [o2r[j] * gi[j] - o2i[j] * gr[j] for j in range(GROUP)]
        fr, fi = transform(cr, ci, tab, False)
        ur = [kr * fr[j] + ki * fi[j] for j in range(GROUP)]
        ui = [kr * fi[j] - ki * fr[j] for j in range(GROUP)]
        nr, ni = transform(ur, ui, tab, True)
        for j in range(GROUP):
            g1r = pr[j][0] * nr[j] + pr[j][1] * ni[j]
            g1i = pr[j][0] * ni[j] - pr[j][1] * nr[j]

            @pl.when(fs[j] < count)
            def _():
                add_back(fs[j], [g1r, g1i, g2r[j], g2i[j]])
        return carry

    group(0, 0)


    if not last:
        copies = [pltpu.make_async_copy(grad, outs[0], sems.at[0])]
        copies[0].start()
        for rb in range(4):
            for cb in range(3):
                ext[rb, cb] = ext[rb, cb] - STEP * grad[rb, cb]
            c = pltpu.make_async_copy(ext.at[rb, pl.ds(0, 3)], outs[1].at[rb], sems.at[1 + rb])
            c.start()
            copies.append(c)
    else:
        out_ref, right_ref, bottom_ref = outs
        copies = [
            pltpu.make_async_copy(grad.at[:, 3], right_ref, sems.at[9]),
            pltpu.make_async_copy(grad.at[3, pl.ds(0, 3)], bottom_ref, sems.at[10]),
        ]
        for c in copies:
            c.start()
        for rb in range(3):
            for cb in range(3):
                ext[rb, cb] = ext[rb, cb] - STEP * grad[rb, cb]
                c = pltpu.make_async_copy(
                    ext.at[rb, cb], out_ref.at[:, pl.ds(rb * B, B), pl.ds(cb * B, B)], sems.at[rb * 3 + cb]
                )
                c.start()
                copies.append(c)
    for c in copies:
        c.wait()


def frame_grads(last, positions, count, pieces, intensity, probe_field, kern, tab):
    anyspec = pl.BlockSpec(memory_space=pl.ANY)
    vmem = pl.BlockSpec(memory_space=pltpu.VMEM)
    hbm = pl.BlockSpec(memory_space=pltpu.HBM)
    smem = pl.BlockSpec(memory_space=pltpu.SMEM)
    shape = lambda *dims: jax.ShapeDtypeStruct(dims, jnp.float32)
    if last:
        outs = [shape(4, 3 * B, 3 * B), shape(4, 4, B, B), shape(3, 4, B, B)]
    else:
        outs = [shape(4, 4, 4, B, B), shape(4, 3, 4, B, B)]
    return pl.pallas_call(
        functools.partial(frames_kernel, last, len(pieces)),
        out_shape=outs,
        in_specs=[smem, smem] + [anyspec if last else hbm] * len(pieces) + [hbm, vmem, vmem, hbm],
        out_specs=[anyspec] * len(outs),
        scratch_shapes=[
            pltpu.VMEM((4, 4, 4, B, B), jnp.float32),
            pltpu.VMEM((4, 4, 4, B, B), jnp.float32),
            pltpu.VMEM((8, B, B), jnp.float32),
            pltpu.VMEM((4, 2 * B, 2 * B), jnp.bfloat16),
            pltpu.SemaphoreType.DMA((24,)),
            pltpu.SemaphoreType.DMA,
        ],
        compiler_params=pltpu.CompilerParams(vmem_limit_bytes=(32 if last else 50) * 1024 * 1024),
        cost_estimate=pl.CostEstimate(flops=2 * 10**9, bytes_accessed=9 * 10**6, transcendentals=0),
        name="last_frames" if last else "frames",
    )(positions, count, *pieces, intensity, probe_field, kern, tab)


def passed_around(x, by):
    places = [(y, z) for y in range(ROWS // RING) for z in range(RING)]
    for step in range(RING - 1):
        pairs = []
        for y, z in places:
            z_to = (z - by) % RING
            y_to = y
            if step == RING - 2:
                start = (z + by * step) % RING
                y_to = y + (start + by) // RING
            if 0 <= y_to < ROWS // RING:
                pairs.append((y * RING + z, y_to * RING + z_to))
        x = lax.ppermute(x, "row", pairs)
    return x


def passed_along(x, axis, by):
    count = lax.axis_size(axis)
    pairs = [(i, i + by) for i in range(count) if 0 <= i + by < count]
    return lax.ppermute(x, axis, pairs)


def local(object_tiles, probe_field, prop_phase, intensity, positions, counts):
    tile = object_tiles.reshape(4, 3 * B, 3 * B)
    count = counts[0, lax.axis_index("col")][None]
    inside = (lax.axis_index("row") < lax.axis_size("row") - 1).astype(jnp.float32)
    kern = jnp.stack([jnp.cos(prop_phase), jnp.sin(prop_phase)])
    tab = jnp.asarray(dft_tables())
    consts = (intensity, probe_field, kern, tab)

    low = passed_along(tile[:, :B, :B], "row", -1)
    bottom = passed_along(tile[:, : B - SHARE, B:], "row", -1)
    rest = passed_around(tile[:, B - SHARE : B, B:], -1)
    right = passed_along(tile[:, :, :B], "col", -1)
    corner = passed_along(low, "col", -1)
    grad, moved = frame_grads(
        False, positions, count, (tile, right, low, bottom, rest, corner), *consts
    )

    cross = passed_along(jnp.stack([grad[0, 3], grad[3, 3]]), "col", 1)
    up = passed_along(grad[0, 1:3], "row", -1)
    down = passed_along(grad[3, 1:3], "row", 1)
    over = passed_along(grad[1:3, 3], "col", 1)
    up_first = passed_along(grad[0, 0] + cross[0], "row", -1)
    down_first = passed_along(grad[3, 0] + cross[1], "row", 1)
    left = moved[1:3, 0] - STEP * over
    side = passed_along(left, "col", -1)
    first = moved[0, 0] - STEP * (cross[0] + down_first)
    low = (moved[3, 0] - STEP * (cross[1] + up_first)) * inside
    ends = passed_along(jnp.stack([first, low]), "col", -1)
    core = moved[1:3, 1:3].reshape(4, 4, B, B)
    top = moved[0, 1:3] - STEP * down
    bottom = (moved[3, 1:3] - STEP * up) * inside
    pieces = (core, top, left, first[None], side, bottom, low[None], ends)
    out, right, under = frame_grads(True, positions, count, pieces, *consts)

    cross = passed_along(right[3], "col", 1)
    down = passed_along(under[1:3, :, : B - SHARE], "row", 1)
    rest = passed_around(under[1:3, :, B - SHARE :], 1)
    down = jnp.concatenate([down, rest], axis=2)
    over = passed_along(right[0:3], "col", 1)
    down_first = passed_along(under[0] + cross, "row", 1)
    top_add = jnp.concatenate([down_first, down[0], down[1]], axis=2)
    left_add = over.transpose(1, 0, 2, 3).reshape(4, 3 * B, B)
    out = out.at[:, :B, :].add(-STEP * top_add)
    out = out.at[:, :, :B].add(-STEP * left_add)
    return out.reshape(object_tiles.shape)


def solution(mesh):
    return jax.shard_map(
        local,
        mesh=mesh,
        in_specs=(
            P(None, None, "row", "col"),
            P(),
            P(),
            P(("row", "col"), None, None),
            P(("row", "col"), None),
            P("row", None),
        ),
        out_specs=P(None, None, "row", "col"),
        check_vma=False,
    )
```
